32 devices in a mesh: parts: 2 (over x), dp: 16 (over z, y, core).
Axes of the slice: x: 2, y: 2, z: 4, core: 2. Of those that a mesh axis runs over, the one named last changes fastest.
Arguments:
- train_grads: bfloat16 [16384, 4096], P(('parts', 'dp')), parts along dimension 0, may hold values from -160 to 160
- query_grads: bfloat16 [768, 4096], P(('parts', 'dp')), parts along dimension 0, may hold values from -0.29882812 to 0.29882812
- in_basis: bfloat16 [4, 32, 32], replicated, may hold values from -1 to 1
- out_basis: bfloat16 [4, 32, 32], replicated, may hold values from -1 to 1
- damping: float32 [2], replicated, may hold values from 0.05 to 1
- layer_group: int32 [4], replicated, may hold values from 0 to 1, as said below
Outputs:
- scores: float32 [16384, 384], P(('parts', 'dp')), parts along dimension 0
The draws below stay inside these ranges and needn't reach their ends.
There are 2 independent parts, one for each index of `parts`. The reference program is written for one: setup_inputs(seed, part) draws one part's arguments, and reference() takes and returns one part's arrays. A program takes and returns all parts, laid end to end along the dimension named above; an argument that names none is the same for every part. Nothing has to cross between parts.
Inputs may be any that keep to these rules, and one draw needn't show every extreme that they name: `layer_group`: every group holds at least one layer.
All inputs are finite; a program needn't handle non-finite values.
Results may differ from the reference program's by a relative error of at most 0.0065.
Values may be sent and summed in bfloat16 or wider, within the bound.
A program may use at most 128 MiB of HBM per device.

```python
import math
import jax
import jax.numpy as jnp
from jax import lax

R = 32
L = 4
NG = 2
TRAIN = 8192
Q = 384


def draw_train_grads(key, part):
    first = jax.random.fold_in(key, 0)
    positions = jnp.arange(TRAIN, dtype=jnp.float32)
    rising = 1.0 + 2.0 * positions / max(TRAIN - 1, 1)
    values = jnp.clip(jax.random.normal(first, (TRAIN, L * R * R), jnp.float32), -6.0, 6.0) * rising[:, None]
    return jnp.clip(values, -160.0, 160.0).astype(jnp.bfloat16)


def draw_layer_group(key, part):
    first, second = jax.random.split(jax.random.fold_in(key, 17))
    chosen = jax.random.randint(first, (L,), 0, NG, dtype=jnp.int32)
    order = jax.random.permutation(second, L)
    chosen = chosen.at[order[:NG]].set(jnp.arange(NG, dtype=jnp.int32))
    return chosen.astype(jnp.int32)


def block_levels(key, extent, pieces, least, high):
    factor_of = 1.0
    for dim, shards_of in pieces:
        draws = jax.random.uniform(jax.random.fold_in(jax.random.fold_in(key, 6), dim), (shards_of,), jnp.float32, least / len(pieces), high / len(pieces))
        factor_of = factor_of * jnp.repeat(jnp.exp(draws), extent[dim] // shards_of).reshape((-1,) + (1,) * (len(extent) - 1 - dim))
    return factor_of


def bell_draw(own_key, extent, deviation, most, shards=(), held_as=jnp.bfloat16):
    values = jax.random.normal(own_key, extent, jnp.float32) * deviation
    if len(shards) > 0:
        values = block_levels(own_key, extent, shards, -0.22, 0.18) * values
    return jnp.clip(values, min=-most, max=most).astype(held_as)


def setup_inputs(seed: int = 0, part: int = 0) -> dict:
    seeds = jax.random.split(jax.random.key(seed), 7)
    part_splits = jax.random.split(jax.random.fold_in(seeds[6], part), 7)
    train_grads = draw_train_grads(jax.random.fold_in(jax.random.fold_in(seeds[6], part), 71), part)
    query_grads = bell_draw(part_splits[1], (Q, L * R * R), 0.05, 0.29882812, ((0, 16),))
    in_basis = bell_draw(seeds[2], (L, R, R), R ** -0.5, 1.0)
    out_basis = bell_draw(seeds[3], (L, R, R), R ** -0.5, 1.0)
    damping = jnp.clip(jnp.exp(jax.random.uniform(seeds[4], (NG,), jnp.float32, math.log(0.05), math.log(1.0))), 0.05, 1.0)
    layer_group = draw_layer_group(jax.random.fold_in(seeds[6], 71), part)
    return {"train_grads": train_grads, "query_grads": query_grads, "in_basis": in_basis, "out_basis": out_basis, "damping": damping, "layer_group": layer_group}


def rotate(grads, in_basis, out_basis):
    rows = grads.shape[0]
    shaped = grads.astype(jnp.float32).reshape(rows, L, R, R)
    inner = jnp.einsum('tlij,ljb->tlib', shaped, in_basis.astype(jnp.float32), precision=lax.Precision.HIGHEST)
    inner = inner.astype(jnp.bfloat16).astype(jnp.float32)
    outer = jnp.einsum('tlib,lia->tlab', inner, out_basis.astype(jnp.float32), precision=lax.Precision.HIGHEST)
    return outer.reshape(rows, L * R * R)


def reference(train_grads, query_grads, in_basis, out_basis, damping, layer_group):
    rotated = rotate(train_grads, in_basis, out_basis)
    corrected = (jnp.sum(rotated * rotated, axis=0) / TRAIN).reshape(L, R * R)
    pick = (layer_group[:, None] == jnp.arange(NG, dtype=jnp.int32)[None, :]).astype(jnp.float32)
    per_layer = jnp.sum(pick * damping[None, :], axis=1)
    denominator = (corrected + per_layer[:, None] * jnp.mean(corrected, axis=1, keepdims=True)).reshape(-1)
    train_rounded = rotated.astype(jnp.bfloat16)
    preconditioned = (rotate(query_grads, in_basis, out_basis) / denominator).astype(jnp.bfloat16)
    return jnp.dot(train_rounded.astype(jnp.float32), preconditioned.astype(jnp.float32).T, precision=lax.Precision.HIGHEST)
```

```python
import functools

import jax
import jax.numpy as jnp
from jax import lax
from jax.experimental import pallas as pl
from jax.experimental.pallas import tpu as pltpu
from jax.sharding import PartitionSpec as P

F32 = jnp.float32
BF16 = jnp.bfloat16
CORES = 2
LINES = 2
TRANS = (((1,), (1,)), ((), ()))


def kernel(
    dp, count, train, query, in_basis, out_basis, damping, layer_group, out,
    rows_in, gathered, basis, rotated, scaled, near, far, inverse,
    train_sem, own_sem, z_send, z_recv, y_send, y_recv, c_send, c_recv,
    near_send, near_recv, far_send, far_recv,
):
    layers, rows, size = rows_in.shape
    width = in_basis.shape[1]
    depth = dp // (CORES * LINES)
    queries = gathered.shape[1] * gathered.shape[2]
    tile = 256
    me = lax.axis_index("dp")
    c = lax.rem(me, CORES)
    y = lax.rem(me // CORES, LINES)
    z = me // (CORES * LINES)

    def device(z_, y_, c_):
        return (z_ * LINES + y_) * CORES + c_

    def behind(k):
        return lax.rem(z + depth - k, depth)

    def ahead(k):
        return lax.rem(z + k, depth)

    other_y = 1 - y
    other_c = 1 - c

    def columns(ch):
        return pl.ds(pl.multiple_of(ch * size, size), size)

    def mate(j):
        return device(z, lax.rem(y + j // CORES, LINES), lax.rem(c + j % CORES, CORES))

    def remote(src, dst, send, recv, to):
        return pltpu.make_async_remote_copy(
            src_ref=src, dst_ref=dst, send_sem=send, recv_sem=recv,
            device_id={"dp": to}, device_id_type=pl.DeviceIdType.MESH,
        )

    def load(l):
        return pltpu.make_async_copy(train.at[:, columns(l)], rows_in.at[l], train_sem.at[l])

    def own(ch):
        return pltpu.make_async_copy(query.at[:, columns(ch)], gathered.at[ch, me], own_sem.at[ch])

    def z_copy(ch, k, slot):
        return remote(query.at[:, columns(ch)], gathered.at[ch, slot], z_send.at[ch, k], z_recv.at[ch, k],
                      device(ahead(k), y, c))

    def y_copy(ch, k, slot):
        return remote(gathered.at[ch, slot], gathered.at[ch, slot], y_send.at[ch, k], y_recv.at[ch, k],
                      device(z, other_y, c))

    def c_copy(ch, line, k, slot):
        return remote(gathered.at[ch, slot], gathered.at[ch, slot], c_send.at[ch, line, k],
                      c_recv.at[ch, line, k], device(z, y, other_c))

    for l in range(layers):
        load(l).start()
    for ch in range(layers):
        own(ch).start()

    barrier = pltpu.get_barrier_semaphore()

    def greet(k, carry):
        pl.semaphore_signal(barrier, inc=1, device_id={"dp": device(ahead(k), y, c)},
                            device_id_type=pl.DeviceIdType.MESH)
        return carry

    lax.fori_loop(1, depth, greet, 0)
    for j in range(1, CORES * LINES):
        pl.semaphore_signal(barrier, inc=1, device_id={"dp": mate(j)}, device_id_type=pl.DeviceIdType.MESH)
    pl.semaphore_wait(barrier, depth - 1 + CORES * LINES - 1)

    def begin(ch, carry):
        def to_z(k, inner):
            z_copy(ch, k, me).start()
            return inner

        lax.fori_loop(1, depth, to_z, 0)
        own(ch).wait()
        y_copy(ch, 0, me).start()
        c_copy(ch, 0, 0, me).start()
        return carry

    lax.fori_loop(0, layers, begin, 0)

    def forward_z(ch):
        def step(k, carry):
            slot = device(behind(k), y, c)
            z_copy(ch, k, slot).wait_recv()
            y_copy(ch, k, slot).start()
            c_copy(ch, 0, k, slot).start()
            return carry

        lax.fori_loop(1, depth, step, 0)

    def forward_y(ch):
        def step(k, carry):
            slot = device(behind(k), other_y, c)
            y_copy(ch, k, slot).wait_recv()
            c_copy(ch, 1, k, slot).start()
            return carry

        lax.fori_loop(0, depth, step, 0)

    def arrive(ch):
        def step(k, carry):
            c_copy(ch, 0, k, device(behind(k), y, other_c)).wait_recv()
            c_copy(ch, 1, k, device(behind(k), other_y, other_c)).wait_recv()
            return carry

        lax.fori_loop(0, depth, step, 0)

    lane = lax.broadcasted_iota(jnp.int32, (width, size), 1)
    line = lax.broadcasted_iota(jnp.int32, (width, size), 0)
    spread_out = jnp.where(lane // width == line, 1.0, 0.0).astype(BF16)
    spread_in = jnp.where(lane % width == line, 1.0, 0.0).astype(BF16)

    def rotate(l, carry):
        outer = jnp.dot(out_basis[l], spread_out, preferred_element_type=F32)
        inner = jnp.dot(in_basis[l], spread_in, preferred_element_type=F32)
        for i in range(width):
            basis[l, i * width:(i + 1) * width, :] = (outer[i:i + 1, :] * inner).astype(BF16)
        load(l).wait()
        for n in range(size // tile):
            cols = slice(n * tile, (n + 1) * tile)
            part = jnp.dot(rows_in[l], basis[l, :, cols], preferred_element_type=F32)
            rotated[l, :, cols] = part
            near[0, l, :, cols] = jnp.sum(part * part, axis=0, keepdims=True)
        return carry

    lax.fori_loop(0, layers, rotate, 0)

    def near_copy(j):
        return remote(near.at[0], near.at[j], near_send.at[j], near_recv.at[j], mate(j))

    def far_copy(k):
        return remote(far.at[0], far.at[k], far_send.at[k], far_recv.at[k], device(ahead(k), y, c))

    for j in range(1, CORES * LINES):
        near_copy(j).start()
    forward_z(0)
    for j in range(1, CORES * LINES):
        near_copy(j).wait_recv()
    far[0] = (near[0] + near[1]) + (near[2] + near[3])

    def send_far(k, carry):
        far_copy(k).start()
        return carry

    lax.fori_loop(1, depth, send_far, 0)
    forward_z(1)
    forward_y(0)

    def take_far(k, total):
        far_copy(k).wait_recv()
        return total + far[k]

    total = lax.fori_loop(1, depth, take_far, far[0])
    corrected = total * (1.0 / count)
    for l in range(layers):
        damp = 0.0
        for g in range(damping.shape[0]):
            damp = damp + jnp.where(layer_group[l] == g, damping[g], 0.0)
        row = corrected[l]
        inverse[l] = 1.0 / (row + damp * jnp.mean(row, axis=1, keepdims=True))

    def back(l):
        scaled[...] = (rotated[l] * inverse[l]).astype(BF16)
        for n in range(size // tile):
            cols = slice(n * tile, (n + 1) * tile)
            part = lax.dot_general(scaled[...], basis[l, cols, :], TRANS, preferred_element_type=F32)
            rows_in[l, :, cols] = part.astype(BF16)

    for ch in range(layers):
        if ch >= 2:
            forward_z(ch)
        if ch >= 1:
            forward_y(ch)
        back(ch)

    for ch in range(layers):
        arrive(ch)
        block = gathered[ch].astype(F32).reshape(queries, size).astype(BF16)
        term = lax.dot_general(rows_in[ch], block, TRANS, preferred_element_type=F32)
        if ch == 0:
            out[...] = term
        else:
            out[...] += term

    def finish(ch, carry):
        def step(k, inner):
            y_copy(ch, k, me).wait_send()
            c_copy(ch, 0, k, me).wait_send()
            c_copy(ch, 1, k, me).wait_send()
            return inner

        def step_z(k, inner):
            z_copy(ch, k, me).wait_send()
            return inner

        lax.fori_loop(0, depth, step, 0)
        lax.fori_loop(1, depth, step_z, 0)
        return carry

    lax.fori_loop(0, layers, finish, 0)
    for j in range(1, CORES * LINES):
        near_copy(j).wait_send()

    def finish_far(k, carry):
        far_copy(k).wait_send()
        return carry

    lax.fori_loop(1, depth, finish_far, 0)


def per_device(dp, train_grads, query_grads, in_basis, out_basis, damping, layer_group):
    layers, width, _ = in_basis.shape
    rows = train_grads.shape[0]
    each = query_grads.shape[0]
    size = width * width
    depth = dp // (CORES * LINES)
    dma = pltpu.SemaphoreType.DMA
    vmem = pl.BlockSpec(memory_space=pltpu.VMEM)
    smem = pl.BlockSpec(memory_space=pltpu.SMEM)
    anywhere = pl.BlockSpec(memory_space=pl.ANY)
    return pl.pallas_call(
        functools.partial(kernel, dp, float(rows * dp)),
        out_shape=jax.ShapeDtypeStruct((rows, each * dp), F32),
        in_specs=[anywhere, anywhere, vmem, vmem, smem, smem],
        out_specs=vmem,
        scratch_shapes=[
            pltpu.VMEM((layers, rows, size), BF16),
            pltpu.VMEM((layers, dp, each, size), BF16),
            pltpu.VMEM((layers, size, size), BF16),
            pltpu.VMEM((layers, rows, size), F32),
            pltpu.VMEM((rows, size), BF16),
            pltpu.VMEM((CORES * LINES, layers, 1, size), F32),
            pltpu.VMEM((depth, layers, 1, size), F32),
            pltpu.VMEM((layers, 1, size), F32),
            dma((layers,)), dma((layers,)),
            dma((layers, depth)), dma((layers, depth)),
            dma((layers, depth)), dma((layers, depth)),
            dma((layers, LINES, depth)), dma((layers, LINES, depth)),
            dma((CORES * LINES,)), dma((CORES * LINES,)),
            dma((depth,)), dma((depth,)),
        ],
        compiler_params=pltpu.CompilerParams(
            collective_id=0, has_side_effects=True, vmem_limit_bytes=56 * 1024 * 1024
        ),
        name="scores",
    )(train_grads, query_grads, in_basis, out_basis, damping, layer_group)


def solution(mesh):
    placed = (P(("parts", "dp"), None), P(("parts", "dp"), None), P(), P(), P(), P())
    return jax.shard_map(
        functools.partial(per_device, mesh.shape["dp"]),
        mesh=mesh, in_specs=placed, out_specs=P(("parts", "dp"), None), check_vma=False,
    )
```

```python
import functools

import jax
import jax.numpy as jnp
from jax import lax
from jax.experimental import pallas as pl
from jax.experimental.pallas import tpu as pltpu
from jax.sharding import PartitionSpec as P

F32 = jnp.float32
BF16 = jnp.bfloat16
CORES = 2
LINES = 2
TRANS = (((1,), (1,)), ((), ()))


def kernel(
    dp, count, train, query, in_basis, out_basis, damping, layer_group, out,
    rows_in, gathered, basis, rotated, scaled, near, far,
    train_sem, own_sem, u_send, u_recv, d_send, d_recv, y_send, y_recv, c_send, c_recv,
    near_send, near_recv, far_send, far_recv,
):
    layers, rows, size = rows_in.shape
    width = in_basis.shape[1]
    depth = dp // (CORES * LINES)
    queries = gathered.shape[1] * gathered.shape[2]
    tile = 256
    me = lax.axis_index("dp")
    c = lax.rem(me, CORES)
    y = lax.rem(me // CORES, LINES)
    z = me // (CORES * LINES)

    def device(z_, y_, c_):
        return (z_ * LINES + y_) * CORES + c_

    def behind(k):
        return lax.rem(z + depth - k, depth)

    def ahead(k):
        return lax.rem(z + k, depth)

    other_y = 1 - y
    other_c = 1 - c

    def columns(ch):
        return pl.ds(pl.multiple_of(ch * size, size), size)

    def mate(j):
        return device(z, lax.rem(y + j // CORES, LINES), lax.rem(c + j % CORES, CORES))

    def remote(src, dst, send, recv, to):
        return pltpu.make_async_remote_copy(
            src_ref=src, dst_ref=dst, send_sem=send, recv_sem=recv,
            device_id={"dp": to}, device_id_type=pl.DeviceIdType.MESH,
        )

    def load(l):
        return pltpu.make_async_copy(train.at[:, columns(l)], rows_in.at[l], train_sem.at[l])

    def own(ch):
        return pltpu.make_async_copy(query.at[:, columns(ch)], gathered.at[ch, me], own_sem.at[ch])

    def up_copy(ch, m, slot):
        return remote(gathered.at[ch, slot], gathered.at[ch, slot], u_send.at[ch, m], u_recv.at[ch, m],
                      device(z + 1, y, c))

    def down_copy(ch, m, slot):
        return remote(gathered.at[ch, slot], gathered.at[ch, slot], d_send.at[ch, m], d_recv.at[ch, m],
                      device(z - 1, y, c))

    def y_copy(ch, k, slot):
        return remote(gathered.at[ch, slot], gathered.at[ch, slot], y_send.at[ch, k], y_recv.at[ch, k],
                      device(z, other_y, c))

    def c_copy(ch, line, k, slot):
        return remote(gathered.at[ch, slot], gathered.at[ch, slot], c_send.at[ch, line, k],
                      c_recv.at[ch, line, k], device(z, y, other_c))

    for l in range(layers):
        load(l).start()
    for ch in range(layers):
        own(ch).start()

    barrier = pltpu.get_barrier_semaphore()

    def greet(k, carry):
        pl.semaphore_signal(barrier, inc=1, device_id={"dp": device(ahead(k), y, c)},
                            device_id_type=pl.DeviceIdType.MESH)
        return carry

    lax.fori_loop(1, depth, greet, 0)
    for j in range(1, CORES * LINES):
        pl.semaphore_signal(barrier, inc=1, device_id={"dp": mate(j)}, device_id_type=pl.DeviceIdType.MESH)
    pl.semaphore_wait(barrier, depth - 1 + CORES * LINES - 1)

    below = z > 0
    above = z < depth - 1

    def begin(ch, carry):
        own(ch).wait()

        @pl.when(above)
        def _():
            up_copy(ch, 1, me).start()

        @pl.when(below)
        def _():
            down_copy(ch, 1, me).start()

        y_copy(ch, 0, me).start()
        c_copy(ch, 0, 0, me).start()
        return carry

    lax.fori_loop(0, layers, begin, 0)

    def hop(step):
        m, ch = step // layers + 1, lax.rem(step, layers)

        @pl.when(z >= m)
        def _():
            slot = device(z - m, y, c)
            up_copy(ch, m, slot).wait_recv()

            @pl.when(above)
            def _():
                up_copy(ch, m + 1, slot).start()

            y_copy(ch, m, slot).start()
            c_copy(ch, 0, m, slot).start()

        @pl.when(z + m < depth)
        def _():
            slot = device(z + m, y, c)
            down_copy(ch, m, slot).wait_recv()

            @pl.when(below)
            def _():
                down_copy(ch, m + 1, slot).start()

            y_copy(ch, depth - m, slot).start()
            c_copy(ch, 0, depth - m, slot).start()

    def cross(step):
        m, ch = step // layers, lax.rem(step, layers)

        @pl.when(z >= m)
        def _():
            slot = device(z - m, other_y, c)
            y_copy(ch, m, slot).wait_recv()
            c_copy(ch, 1, m, slot).start()

        @pl.when(jnp.logical_and(m > 0, z + m < depth))
        def _():
            slot = device(z + m, other_y, c)
            y_copy(ch, depth - m, slot).wait_recv()
            c_copy(ch, 1, depth - m, slot).start()

    def run(move, start, count_):
        def step(i, carry):
            move(start + i)
            return carry

        lax.fori_loop(0, count_, step, 0)

    def arrive(ch):
        def step(k, carry):
            c_copy(ch, 0, k, device(behind(k), y, other_c)).wait_recv()
            c_copy(ch, 1, k, device(behind(k), other_y, other_c)).wait_recv()
            return carry

        lax.fori_loop(0, depth, step, 0)

    lane = lax.broadcasted_iota(jnp.int32, (width, size), 1)
    line = lax.broadcasted_iota(jnp.int32, (width, size), 0)
    spread_out = jnp.where(lane // width == line, 1.0, 0.0).astype(BF16)
    spread_in = jnp.where(lane % width == line, 1.0, 0.0).astype(BF16)

    def near_copy(j, l):
        return remote(near.at[0, l], near.at[j, l], near_send.at[j, l], near_recv.at[j, l], mate(j))

    def far_copy(k, l):
        return remote(far.at[0, l], far.at[k, l], far_send.at[k, l], far_recv.at[k, l], device(ahead(k), y, c))

    def send_far(l):
        total = near[0, l]
        for j in range(1, CORES * LINES):
            near_copy(j, l).wait_recv()
            total = total + near[j, l]
        far[0, l] = total

        def step(k, carry):
            far_copy(k, l).start()
            return carry

        lax.fori_loop(1, depth, step, 0)

    def take_far(l):
        def step(k, total):
            far_copy(k, l).wait_recv()
            return total + far[k, l]

        row = lax.fori_loop(1, depth, step, far[0, l]) * (1.0 / count)
        damp = 0.0
        for g in range(damping.shape[0]):
            damp = damp + jnp.where(layer_group[l] == g, damping[g], 0.0)
        return 1.0 / (row + damp * jnp.mean(row, axis=1, keepdims=True))

    hops = (depth - 1) * 2 // 3
    late_hops = depth - 1 - hops
    crosses = depth // 4
    late_crosses = depth - crosses

    def rotate(l, carry):
        outer = jnp.dot(out_basis[l], spread_out, preferred_element_type=F32)
        inner = jnp.dot(in_basis[l], spread_in, preferred_element_type=F32)
        for i in range(width):
            basis[l, i * width:(i + 1) * width, :] = (outer[i:i + 1, :] * inner).astype(BF16)
        load(l).wait()
        for n in range(size // tile):
            cols = slice(n * tile, (n + 1) * tile)
            part = jnp.dot(rows_in[l], basis[l, :, cols], preferred_element_type=F32)
            rotated[l, :, cols] = part
            near[0, l, :, cols] = jnp.sum(part * part, axis=0, keepdims=True)
        for j in range(1, CORES * LINES):
            near_copy(j, l).start()
        run(hop, l * hops, hops)

        @pl.when(l > 0)
        def _():
            send_far(l - 1)

        run(cross, l * crosses, crosses)
        return carry

    lax.fori_loop(0, layers, rotate, 0)
    send_far(layers - 1)

    def back(l, carry):
        scaled[...] = (rotated[l] * take_far(l)).astype(BF16)
        for n in range(size // tile):
            cols = slice(n * tile, (n + 1) * tile)
            part = lax.dot_general(scaled[...], basis[l, cols, :], TRANS, preferred_element_type=F32)
            rows_in[l, :, cols] = part.astype(BF16)
        run(hop, layers * hops + l * late_hops, late_hops)
        run(cross, layers * crosses + l * late_crosses, late_crosses)
        return carry

    lax.fori_loop(0, layers, back, 0)

    for ch in range(layers):
        arrive(ch)
        block = gathered[ch].astype(F32).reshape(queries, size).astype(BF16)
        term = lax.dot_general(rows_in[ch], block, TRANS, preferred_element_type=F32)
        if ch == 0:
            out[...] = term
        else:
            out[...] += term

    def finish(ch, carry):
        def step(k, inner):
            y_copy(ch, k, me).wait_send()
            c_copy(ch, 0, k, me).wait_send()
            c_copy(ch, 1, k, me).wait_send()
            return inner

        def step_z(m, inner):
            @pl.when(jnp.logical_and(above, z + 1 >= m))
            def _():
                up_copy(ch, m, me).wait_send()

            @pl.when(jnp.logical_and(below, z - 1 + m < depth))
            def _():
                down_copy(ch, m, me).wait_send()

            far_copy(m, ch).wait_send()
            return inner

        lax.fori_loop(0, depth, step, 0)
        lax.fori_loop(1, depth, step_z, 0)
        for j in range(1, CORES * LINES):
            near_copy(j, ch).wait_send()
        return carry

    lax.fori_loop(0, layers, finish, 0)


def per_device(dp, train_grads, query_grads, in_basis, out_basis, damping, layer_group):
    layers, width, _ = in_basis.shape
    rows = train_grads.shape[0]
    each = query_grads.shape[0]
    size = width * width
    depth = dp // (CORES * LINES)
    dma = pltpu.SemaphoreType.DMA
    vmem = pl.BlockSpec(memory_space=pltpu.VMEM)
    smem = pl.BlockSpec(memory_space=pltpu.SMEM)
    anywhere = pl.BlockSpec(memory_space=pl.ANY)
    return pl.pallas_call(
        functools.partial(kernel, dp, float(rows * dp)),
        out_shape=jax.ShapeDtypeStruct((rows, each * dp), F32),
        in_specs=[anywhere, anywhere, vmem, vmem, smem, smem],
        out_specs=vmem,
        scratch_shapes=[
            pltpu.VMEM((layers, rows, size), BF16),
            pltpu.VMEM((layers, dp, each, size), BF16),
            pltpu.VMEM((layers, size, size), BF16),
            pltpu.VMEM((layers, rows, size), F32),
            pltpu.VMEM((rows, size), BF16),
            pltpu.VMEM((CORES * LINES, layers, 1, size), F32),
            pltpu.VMEM((depth, layers, 1, size), F32),
            dma((layers,)), dma((layers,)),
            dma((layers, depth)), dma((layers, depth)),
            dma((layers, depth)), dma((layers, depth)),
            dma((layers, depth)), dma((layers, depth)),
            dma((layers, LINES, depth)), dma((layers, LINES, depth)),
            dma((CORES * LINES, layers)), dma((CORES * LINES, layers)),
            dma((depth, layers)), dma((depth, layers)),
        ],
        compiler_params=pltpu.CompilerParams(
            collective_id=0, has_side_effects=True, vmem_limit_bytes=56 * 1024 * 1024
        ),
        name="scores",
    )(train_grads, query_grads, in_basis, out_basis, damping, layer_group)


def solution(mesh):
    placed = (P(("parts", "dp"), None), P(("parts", "dp"), None), P(), P(), P(), P())
    return jax.shard_map(
        functools.partial(per_device, mesh.shape["dp"]),
        mesh=mesh, in_specs=placed, out_specs=P(("parts", "dp"), None), check_vma=False,
    )
```

```python
import functools

import jax
import jax.numpy as jnp
from jax import lax
from jax.experimental import pallas as pl
from jax.experimental.pallas import tpu as pltpu
from jax.sharding import PartitionSpec as P

F32 = jnp.float32
BF16 = jnp.bfloat16
CORES = 2
LINES = 2
TRANS = (((1,), (1,)), ((), ()))


def kernel(
    dp, count, train, query, in_basis, out_basis, damping, layer_group, out,
    rows_in, gathered, basis, rotated, scaled, near, far,
    train_sem, own_sem, u_send, u_recv, d_send, d_recv, y_send, y_recv, c_send, c_recv,
    near_send, near_recv, far_send, far_recv,
):
    layers, rows, size = rows_in.shape
    width = in_basis.shape[1]
    depth = dp // (CORES * LINES)
    queries = gathered.shape[1] * gathered.shape[2]
    tile = 256
    me = lax.axis_index("dp")
    c = lax.rem(me, CORES)
    y = lax.rem(me // CORES, LINES)
    z = me // (CORES * LINES)

    def device(z_, y_, c_):
        return (z_ * LINES + y_) * CORES + c_

    def behind(k):
        return lax.rem(z + depth - k, depth)

    def ahead(k):
        return lax.rem(z + k, depth)

    other_y = 1 - y
    other_c = 1 - c

    def columns(ch):
        return pl.ds(pl.multiple_of(ch * size, size), size)

    def mate(j):
        return device(z, lax.rem(y + j // CORES, LINES), lax.rem(c + j % CORES, CORES))

    def remote(src, dst, send, recv, to):
        return pltpu.make_async_remote_copy(
            src_ref=src, dst_ref=dst, send_sem=send, recv_sem=recv,
            device_id={"dp": to}, device_id_type=pl.DeviceIdType.MESH,
        )

    def load(l):
        return pltpu.make_async_copy(train.at[:, columns(l)], rows_in.at[l], train_sem.at[l])

    def own(ch):
        return pltpu.make_async_copy(query.at[:, columns(ch)], gathered.at[ch, me], own_sem.at[ch])

    def up_copy(ch, m, slot):
        return remote(gathered.at[ch, slot], gathered.at[ch, slot], u_send.at[ch, m], u_recv.at[ch, m],
                      device(z + 1, y, c))

    def down_copy(ch, m, slot):
        return remote(gathered.at[ch, slot], gathered.at[ch, slot], d_send.at[ch, m], d_recv.at[ch, m],
                      device(z - 1, y, c))

    def y_copy(ch, k, slot):
        return remote(gathered.at[ch, slot], gathered.at[ch, slot], y_send.at[ch, k], y_recv.at[ch, k],
                      device(z, other_y, c))

    def c_copy(ch, line, k, slot):
        return remote(gathered.at[ch, slot], gathered.at[ch, slot], c_send.at[ch, line, k],
                      c_recv.at[ch, line, k], device(z, y, other_c))

    for l in range(layers):
        load(l).start()
    for ch in range(layers):
        own(ch).start()

    barrier = pltpu.get_barrier_semaphore()

    def greet(k, carry):
        pl.semaphore_signal(barrier, inc=1, device_id={"dp": device(ahead(k), y, c)},
                            device_id_type=pl.DeviceIdType.MESH)
        return carry

    lax.fori_loop(1, depth, greet, 0)
    for j in range(1, CORES * LINES):
        pl.semaphore_signal(barrier, inc=1, device_id={"dp": mate(j)}, device_id_type=pl.DeviceIdType.MESH)
    pl.semaphore_wait(barrier, depth - 1 + CORES * LINES - 1)

    below = z > 0
    above = z < depth - 1

    def begin(ch, carry):
        own(ch).wait()

        @pl.when(above)
        def _():
            up_copy(ch, 1, me).start()

        @pl.when(below)
        def _():
            down_copy(ch, 1, me).start()

        y_copy(ch, 0, me).start()
        c_copy(ch, 0, 0, me).start()
        return carry

    lax.fori_loop(0, layers, begin, 0)

    def hop(step):
        m, ch = step // layers + 1, lax.rem(step, layers)

        @pl.when(z >= m)
        def _():
            slot = device(z - m, y, c)
            up_copy(ch, m, slot).wait_recv()

            @pl.when(above)
            def _():
                up_copy(ch, m + 1, slot).start()

            y_copy(ch, m, slot).start()
            c_copy(ch, 0, m, slot).start()

        @pl.when(z + m < depth)
        def _():
            slot = device(z + m, y, c)
            down_copy(ch, m, slot).wait_recv()

            @pl.when(below)
            def _():
                down_copy(ch, m + 1, slot).start()

            y_copy(ch, depth - m, slot).start()
            c_copy(ch, 0, depth - m, slot).start()

    def cross(step):
        m, ch = step // layers, lax.rem(step, layers)

        @pl.when(z >= m)
        def _():
            slot = device(z - m, other_y, c)
            y_copy(ch, m, slot).wait_recv()
            c_copy(ch, 1, m, slot).start()

        @pl.when(jnp.logical_and(m > 0, z + m < depth))
        def _():
            slot = device(z + m, other_y, c)
            y_copy(ch, depth - m, slot).wait_recv()
            c_copy(ch, 1, depth - m, slot).start()

    def run(move, start, count_):
        def step(i, carry):
            move(start + i)
            return carry

        lax.fori_loop(0, count_, step, 0)

    def arrive(ch):
        def step(k, carry):
            c_copy(ch, 0, k, device(behind(k), y, other_c)).wait_recv()
            c_copy(ch, 1, k, device(behind(k), other_y, other_c)).wait_recv()
            return carry

        lax.fori_loop(0, depth, step, 0)

    lane = lax.broadcasted_iota(jnp.int32, (width, size), 1)
    line = lax.broadcasted_iota(jnp.int32, (width, size), 0)
    spread_out = jnp.where(lane // width == line, 1.0, 0.0).astype(BF16)
    spread_in = jnp.where(lane % width == line, 1.0, 0.0).astype(BF16)

    def near_copy(j, l):
        return remote(near.at[0, l], near.at[j, l], near_send.at[j, l], near_recv.at[j, l], mate(j))

    def far_copy(k, l):
        return remote(far.at[0, l], far.at[k, l], far_send.at[k, l], far_recv.at[k, l], device(ahead(k), y, c))

    def send_far(l):
        total = near[0, l]
        for j in range(1, CORES * LINES):
            near_copy(j, l).wait_recv()
            total = total + near[j, l]
        far[0, l] = total

        def step(k, carry):
            far_copy(k, l).start()
            return carry

        lax.fori_loop(1, depth, step, 0)

    def take_far(l):
        def step(k, total):
            far_copy(k, l).wait_recv()
            return total + far[k, l]

        row = lax.fori_loop(1, depth, step, far[0, l]) * (1.0 / count)
        damp = 0.0
        for g in range(damping.shape[0]):
            damp = damp + jnp.where(layer_group[l] == g, damping[g], 0.0)
        return 1.0 / (row + damp * jnp.mean(row, axis=1, keepdims=True))

    hops = depth - 1
    late_hops = depth - 1 - hops
    crosses = depth // 2
    late_crosses = depth - crosses

    def rotate(l, carry):
        outer = jnp.dot(out_basis[l], spread_out, preferred_element_type=F32)
        inner = jnp.dot(in_basis[l], spread_in, preferred_element_type=F32)
        for i in range(width):
            basis[l, i * width:(i + 1) * width, :] = (outer[i:i + 1, :] * inner).astype(BF16)
        load(l).wait()
        for n in range(size // tile):
            cols = slice(n * tile, (n + 1) * tile)
            part = jnp.dot(rows_in[l], basis[l, :, cols], preferred_element_type=F32)
            rotated[l, :, cols] = part
            near[0, l, :, cols] = jnp.sum(part * part, axis=0, keepdims=True)
        for j in range(1, CORES * LINES):
            near_copy(j, l).start()
        run(hop, l * hops, hops)

        @pl.when(l > 0)
        def _():
            send_far(l - 1)

        run(cross, l * crosses, crosses)
        return carry

    lax.fori_loop(0, layers, rotate, 0)
    send_far(layers - 1)

    def back(l, carry):
        scaled[...] = (rotated[l] * take_far(l)).astype(BF16)
        for n in range(size // tile):
            cols = slice(n * tile, (n + 1) * tile)
            part = lax.dot_general(scaled[...], basis[l, cols, :], TRANS, preferred_element_type=F32)
            rows_in[l, :, cols] = part.astype(BF16)
        run(hop, layers * hops + l * late_hops, late_hops)
        run(cross, layers * crosses + l * late_crosses, late_crosses)
        return carry

    lax.fori_loop(0, layers, back, 0)

    for ch in range(layers):
        arrive(ch)
        block = gathered[ch].astype(F32).reshape(queries, size).astype(BF16)
        term = lax.dot_general(rows_in[ch], block, TRANS, preferred_element_type=F32)
        if ch == 0:
            out[...] = term
        else:
            out[...] += term

    def finish(ch, carry):
        def step(k, inner):
            y_copy(ch, k, me).wait_send()
            c_copy(ch, 0, k, me).wait_send()
            c_copy(ch, 1, k, me).wait_send()
            return inner

        def step_z(m, inner):
            @pl.when(jnp.logical_and(above, z + 1 >= m))
            def _():
                up_copy(ch, m, me).wait_send()

            @pl.when(jnp.logical_and(below, z - 1 + m < depth))
            def _():
                down_copy(ch, m, me).wait_send()

            far_copy(m, ch).wait_send()
            return inner

        lax.fori_loop(0, depth, step, 0)
        lax.fori_loop(1, depth, step_z, 0)
        for j in range(1, CORES * LINES):
            near_copy(j, ch).wait_send()
        return carry

    lax.fori_loop(0, layers, finish, 0)


def per_device(dp, train_grads, query_grads, in_basis, out_basis, damping, layer_group):
    layers, width, _ = in_basis.shape
    rows = train_grads.shape[0]
    each = query_grads.shape[0]
    size = width * width
    depth = dp // (CORES * LINES)
    dma = pltpu.SemaphoreType.DMA
    vmem = pl.BlockSpec(memory_space=pltpu.VMEM)
    smem = pl.BlockSpec(memory_space=pltpu.SMEM)
    anywhere = pl.BlockSpec(memory_space=pl.ANY)
    return pl.pallas_call(
        functools.partial(kernel, dp, float(rows * dp)),
        out_shape=jax.ShapeDtypeStruct((rows, each * dp), F32),
        in_specs=[anywhere, anywhere, vmem, vmem, smem, smem],
        out_specs=vmem,
        scratch_shapes=[
            pltpu.VMEM((layers, rows, size), BF16),
            pltpu.VMEM((layers, dp, each, size), BF16),
            pltpu.VMEM((layers, size, size), BF16),
            pltpu.VMEM((layers, rows, size), F32),
            pltpu.VMEM((rows, size), BF16),
            pltpu.VMEM((CORES * LINES, layers, 1, size), F32),
            pltpu.VMEM((depth, layers, 1, size), F32),
            dma((layers,)), dma((layers,)),
            dma((layers, depth)), dma((layers, depth)),
            dma((layers, depth)), dma((layers, depth)),
            dma((layers, depth)), dma((layers, depth)),
            dma((layers, LINES, depth)), dma((layers, LINES, depth)),
            dma((CORES * LINES, layers)), dma((CORES * LINES, layers)),
            dma((depth, layers)), dma((depth, layers)),
        ],
        compiler_params=pltpu.CompilerParams(
            collective_id=0, has_side_effects=True, vmem_limit_bytes=56 * 1024 * 1024
        ),
        name="scores",
    )(train_grads, query_grads, in_basis, out_basis, damping, layer_group)


def solution(mesh):
    placed = (P(("parts", "dp"), None), P(("parts", "dp"), None), P(), P(), P(), P())
    return jax.shard_map(
        functools.partial(per_device, mesh.shape["dp"]),
        mesh=mesh, in_specs=placed, out_specs=P(("parts", "dp"), None), check_vma=False,
    )
```
